32 devices in a mesh: groups: 2 (over y), replica: 4 (over x, core), tensor: 4 (over z).
Axes of the slice: x: 2, y: 2, z: 4, core: 2. Of those that a mesh axis runs over, the one named last changes fastest.
Arguments:
- hidden: bfloat16 [2, 64, 8192], P(None, ('groups', 'replica')), parts along dimension 1, may hold values from -64 to 64
- frozen_query: bfloat16 [2, 64, 8192], P(None, ('groups', 'replica'), 'tensor'), parts along dimension 1, may hold values from -6 to 6
- frozen_key_value: bfloat16 [2, 2, 64, 1024], P(None, None, ('groups', 'replica')), parts along dimension 2, may hold values from -8 to 8
- cache_keys: bfloat16 [64, 64, 512, 128], P(('groups', 'replica'), 'tensor'), parts along dimension 0, may hold values from -12 to 12
- cache_values: bfloat16 [64, 64, 512, 128], P(('groups', 'replica'), 'tensor'), parts along dimension 0, may hold values from -6 to 6
- lengths: int32 [64], P(('groups', 'replica')), parts along dimension 0, may hold values from 128 to 512, as said below
- out_weight: bfloat16 [8192, 8192], P('tensor'), may hold values from -0.75 to 0.75
- down_qkv: bfloat16 [6, 8192, 64], P('groups', 'tensor', 'replica'), parts along dimension 0, may hold values from -0.0625 to 0.0625
- query_up_factor: bfloat16 [128, 8192], P(('groups', 'replica'), 'tensor'), parts along dimension 0, may hold values from -0.75 to 0.75
- key_value_up_factor: bfloat16 [2, 128, 1024], P(None, ('groups', 'replica')), parts along dimension 1, may hold values from -0.75 to 0.75
- output_down_factor: bfloat16 [16384, 64], P(('groups', 'tensor'), 'replica'), parts along dimension 0, may hold values from -0.5 to 0.5
- output_up_factor: bfloat16 [128, 8192], P(('groups', 'replica'), 'tensor'), parts along dimension 0, may hold values from -0.75 to 0.75
- norm_gain: bfloat16 [8192], replicated, may hold values from 0.5 to 1.5
Outputs:
- residual_out: bfloat16 [2, 64, 8192], P(None, ('groups', 'replica'), 'tensor'), parts along dimension 1
- normed_out: bfloat16 [2, 64, 8192], P(None, ('groups', 'replica')), parts along dimension 1
The draws below stay inside these ranges and needn't reach their ends.
There are 2 independent parts, one for each index of `groups`. The reference program is written for one: setup_inputs(seed, part) draws one part's arguments, and reference() takes and returns one part's arrays. A program takes and returns all parts, laid end to end along the dimension named above; an argument that names none is the same for every part. Nothing has to cross between parts.
Inputs may be any that keep to these rules, and one draw needn't show every extreme that they name: `lengths`: some row of the 32 has all 512 slots live.
All inputs are finite; a program needn't handle non-finite values.
Results may differ from the reference program's by a relative error of at most 0.0068.
Values may be sent and summed in bfloat16 or wider, within the bound.
A program may use at most 192 MiB of HBM per device.

```python
import math
import jax
import jax.numpy as jnp
from jax import lax

D = 8192
HEADS = 64
KV = 8
HD = 128
RANK = 64
STEPS = 2
LEN = 512
BATCH = 32


def draw_frozen_query(key, part):
    key = jax.random.fold_in(key, 11)
    values = jnp.clip(jax.random.normal(key, (STEPS, BATCH, HEADS, HD), jnp.float32), -6.0, 6.0)
    return values.reshape(STEPS, BATCH, HEADS * HD).astype(jnp.bfloat16)


def draw_cache_keys(key, part):
    key = jax.random.fold_in(key, 12)
    keys_a = jax.random.fold_in(key, 0)
    drawn = jnp.clip(jax.random.normal(keys_a, (BATCH, HEADS, LEN, HD), jnp.float32), -6.0, 6.0)
    return drawn.astype(jnp.bfloat16)


def draw_hidden(key, part):
    key = jax.random.fold_in(key, 13)
    keys_a, keys_b, keys_c = jax.random.split(key, 3)
    columns = jnp.arange(D, dtype=jnp.float32) / (D - 1)
    values = jnp.clip(jax.random.normal(keys_a, (STEPS, BATCH, D), jnp.float32), -4.0, 4.0)
    rising = 3.0 ** columns
    column_scale = rising * jnp.exp(jax.random.uniform(keys_b, (D,), jnp.float32, 0.0, math.log(4.0)))
    row_scale = jnp.exp(jax.random.uniform(keys_c, (STEPS, BATCH, 1), jnp.float32, 0.0, math.log(10.0)))
    return (values * row_scale * column_scale * 0.1).astype(jnp.bfloat16)


def draw_lengths(key, part):
    key = jax.random.fold_in(key, 14)
    keys_a, keys_b = jax.random.split(key)
    shortest = max(4, LEN // 4)
    drawn_lengths = jax.random.randint(keys_a, (BATCH,), shortest, LEN + 1)
    longest_row = jax.random.randint(keys_b, (), 0, BATCH)
    return drawn_lengths.at[longest_row].set(LEN).astype(jnp.int32)


def spiked(values, rng, source, target, blocks, factor):
    owner, partner = [(jnp.arange(values.shape[axis_at]) // (values.shape[axis_at] // blocks)).reshape([-1 if axis == axis_at else 1 for axis in range(values.ndim)]) for axis_at in (source, target)]
    chosen = jax.random.permutation(rng, blocks)[partner]
    strong = (owner == chosen) | (owner == (partner + blocks // 2) % blocks)
    return jnp.where(strong, factor * values, values)


def shard_levels(own_key, dims, shards, smallest, top_value):
    def one(axis_at, parts):
        steps = jax.random.uniform(jax.random.fold_in(jax.random.fold_in(own_key, 6), axis_at), (parts,), jnp.float32, smallest / len(shards), top_value / len(shards))
        return jnp.repeat(jnp.exp(steps), dims[axis_at] // parts).reshape((-1,) + (1,) * (len(dims) - axis_at - 1))

    loudness = one(*shards[0])
    for cut in shards[1:]:
        loudness = loudness * one(*cut)
    return loudness


def scatter_about(key, extent, width, limit, cuts=(), held_as=jnp.bfloat16):
    entries = jax.random.normal(key, extent, jnp.float32) * width
    if len(cuts) > 0:
        entries = shard_levels(key, extent, cuts, -0.22, 0.18) * entries
    return jnp.clip(entries, min=-limit, max=limit).astype(held_as)


def bell_draw_with(stream_key, shape, deviation, limit, cuts, heavy, kind=jnp.bfloat16):
    array = deviation * jax.random.normal(stream_key, shape, jnp.float32)
    if cuts:
        array = array * shard_levels(stream_key, shape, cuts, -0.22, 0.18)
    return jnp.clip(spiked(array, jax.random.fold_in(stream_key, 3), *heavy), -limit, limit).astype(kind)


def setup_inputs(seed: int = 0, part: int = 0) -> dict:
    seeds = jax.random.split(jax.random.key(seed), 14)
    part_splits = jax.random.split(jax.random.fold_in(seeds[13], part), 14)
    hidden = draw_hidden(jax.random.fold_in(jax.random.fold_in(seeds[13], part), 71), part)
    frozen_query = draw_frozen_query(jax.random.fold_in(jax.random.fold_in(seeds[13], part), 71), part)
    frozen_key_value = scatter_about(part_splits[2], (2, STEPS, BATCH, KV * HD), 2.0, 8.0, ((2, 4),))
    cache_keys = draw_cache_keys(jax.random.fold_in(jax.random.fold_in(seeds[13], part), 71), part)
    cache_values = scatter_about(part_splits[4], (BATCH, HEADS, LEN, HD), 1.0, 6.0, ((0, 4), (1, 4)))
    lengths = draw_lengths(jax.random.fold_in(jax.random.fold_in(seeds[13], part), 71), part)
    out_weight = bell_draw_with(seeds[6], (HEADS * HD, D), HD ** -0.5, 0.75, ((0, 4),), (0, 1, 4, 2.0))
    down_qkv = scatter_about(part_splits[7], (3, D, RANK), D ** -0.5, 0.0625, ((1, 4), (2, 4)))
    query_up_factor = scatter_about(part_splits[8], (RANK, HEADS * HD), RANK ** -0.5, 0.75, ((0, 4), (1, 4)))
    key_value_up_factor = scatter_about(part_splits[9], (2, RANK, KV * HD), RANK ** -0.5, 0.75, ((1, 4),))
    output_down_factor = scatter_about(part_splits[10], (HEADS * HD, RANK), HD ** -0.5, 0.5, ((0, 4), (1, 4)))
    output_up_factor = scatter_about(part_splits[11], (RANK, D), RANK ** -0.5, 0.75, ((0, 4), (1, 4)))
    norm_gain = jnp.clip(1.0 + 0.1 * jax.random.normal(seeds[12], (D,), jnp.float32), 0.5, 1.5).astype(jnp.bfloat16)
    return dict(hidden=hidden, frozen_query=frozen_query, frozen_key_value=frozen_key_value, cache_keys=cache_keys, cache_values=cache_values, lengths=lengths, out_weight=out_weight, down_qkv=down_qkv, query_up_factor=query_up_factor, key_value_up_factor=key_value_up_factor, output_down_factor=output_down_factor, output_up_factor=output_up_factor, norm_gain=norm_gain)


EPSILON = 1e-06
ADAPTER_SCALING = 0.25
NEG_FILL = -1e+30

def rms_scale(values):
    return lax.rsqrt(lax.optimization_barrier(jnp.mean(values * values, axis=-1, keepdims=True)) + EPSILON)

def reference(hidden, frozen_query, frozen_key_value, cache_keys, cache_values, lengths, out_weight, down_qkv, query_up_factor, key_value_up_factor, output_down_factor, output_up_factor, norm_gain):
    step_count = hidden.shape[0]
    row_count = hidden.shape[1]
    hidden_state = hidden.astype(jnp.float32)
    normed_in = (hidden_state * rms_scale(hidden_state)).astype(jnp.bfloat16)
    lowrank_activity = jnp.einsum('sbd,pdr->sbpr', normed_in.astype(jnp.float32), down_qkv.astype(jnp.float32)).astype(jnp.bfloat16)
    lowrank_float = lowrank_activity.astype(jnp.float32)
    query_correction = jnp.einsum('huo,oa->hua', lowrank_float[:, :, 0], query_up_factor.astype(jnp.float32))
    query_vectors = (frozen_query.astype(jnp.float32) + ADAPTER_SCALING * query_correction).astype(jnp.bfloat16)
    query_vectors = query_vectors.reshape(step_count, row_count, HEADS, HD)
    key_correction = jnp.einsum('huo,oa->hua', lowrank_float[:, :, 1], key_value_up_factor[0].astype(jnp.float32))
    value_correction = jnp.einsum('huo,oa->hua', lowrank_float[:, :, 2], key_value_up_factor[1].astype(jnp.float32))
    appended_keys = (frozen_key_value[0].astype(jnp.float32) + ADAPTER_SCALING * key_correction).astype(jnp.bfloat16)
    appended_values = (frozen_key_value[1].astype(jnp.float32) + ADAPTER_SCALING * value_correction).astype(jnp.bfloat16)
    group_size = HEADS // KV
    appended_keys = jnp.repeat(appended_keys.reshape(step_count, row_count, KV, HD), group_size, axis=2)
    appended_values = jnp.repeat(appended_values.reshape(step_count, row_count, KV, HD), group_size, axis=2)
    positions = jnp.arange(LEN)
    causal = jnp.arange(step_count)[None, :] <= jnp.arange(step_count)[:, None]

    def attend_row(row_inputs):
        row_queries, row_keys, row_values, row_length, row_new_keys, row_new_values = row_inputs
        query_float = row_queries.astype(jnp.float32)
        cache_scores = jnp.einsum('shd,hpd->shp', query_float, row_keys.astype(jnp.float32)) / math.sqrt(HD)
        cache_scores = jnp.where(positions[None, None, :] < row_length, cache_scores, NEG_FILL)
        fresh_scores = jnp.einsum('shd,thd->sht', query_float, row_new_keys.astype(jnp.float32)) / math.sqrt(HD)
        fresh_scores = jnp.where(causal[:, None, :], fresh_scores, NEG_FILL)
        highest = jnp.maximum(lax.optimization_barrier(jnp.max(cache_scores, axis=-1)), lax.optimization_barrier(jnp.max(fresh_scores, axis=-1)))[..., None]
        cache_exp = jnp.exp(cache_scores - highest)
        fresh_exp = jnp.exp(fresh_scores - highest)
        denominator = lax.optimization_barrier(jnp.sum(cache_exp, axis=-1, keepdims=True)) + lax.optimization_barrier(jnp.sum(fresh_exp, axis=-1, keepdims=True))
        cache_weights = (cache_exp / denominator).astype(jnp.bfloat16)
        fresh_weights = (fresh_exp / denominator).astype(jnp.bfloat16)
        mixed = jnp.einsum('shp,hpd->shd', cache_weights.astype(jnp.float32), row_values.astype(jnp.float32))
        mixed = mixed + jnp.einsum('sht,thd->shd', fresh_weights.astype(jnp.float32), row_new_values.astype(jnp.float32))
        return mixed.astype(jnp.bfloat16)
    attention_result = lax.map(attend_row, (jnp.moveaxis(query_vectors, 1, 0), cache_keys, cache_values, lengths, jnp.moveaxis(appended_keys, 1, 0), jnp.moveaxis(appended_values, 1, 0)))
    attention_result = jnp.moveaxis(attention_result, 0, 1).reshape(step_count, row_count, HEADS * HD)
    attention_result_float = attention_result.astype(jnp.float32)
    lowrank_output = jnp.einsum('njk,ko->njo', attention_result_float, output_down_factor.astype(jnp.float32))
    frozen_output = jnp.einsum('sbc,cd->sbd', attention_result_float, out_weight.astype(jnp.float32))
    block_result = frozen_output + ADAPTER_SCALING * jnp.einsum('hwt,tm->hwm', lowrank_output, output_up_factor.astype(jnp.float32), precision=lax.Precision.HIGHEST)
    refreshed_state = hidden_state + block_result
    residual_out = refreshed_state.astype(jnp.bfloat16)
    normed_out = (refreshed_state * rms_scale(refreshed_state) * norm_gain.astype(jnp.float32)).astype(jnp.bfloat16)
    return (residual_out, normed_out)
```

```python
import functools
import math

import jax
import jax.numpy as jnp
from jax import lax
from jax.experimental import pallas as pl
from jax.experimental.pallas import tpu as pltpu
from jax.sharding import PartitionSpec as P

HEADS = 64
KV = 8
HD = 128


EPSILON = 1e-06
ADAPTER_SCALING = 0.25
NEG_FILL = -1e30


def rms_scale(values):
    return lax.rsqrt(jnp.mean(values * values, axis=-1, keepdims=True) + EPSILON)


def body(
    hidden,
    frozen_query,
    frozen_key_value,
    cache_keys,
    cache_values,
    lengths,
    out_weight,
    down_qkv,
    query_up_factor,
    key_value_up_factor,
    output_down_factor,
    output_up_factor,
    norm_gain,
):
    tensor_rank = lax.axis_index("tensor")
    tensor_count = lax.axis_size("tensor")
    step_count = hidden.shape[0]
    row_count = hidden.shape[1]
    down_rank, query_up_columns, up_kv_full, output_down_rows, up_o_cols = (
        lax.all_gather(down_qkv, "replica", axis=2, tiled=True),
        lax.all_gather(query_up_factor, "replica", axis=0, tiled=True),
        lax.all_gather(key_value_up_factor, "replica", axis=1, tiled=True),
        lax.all_gather(output_down_factor, "replica", axis=1, tiled=True),
        lax.all_gather(output_up_factor, "replica", axis=0, tiled=True),
    )
    hidden_state = hidden.astype(jnp.float32)
    normed_in = (hidden_state * rms_scale(hidden_state)).astype(jnp.bfloat16)
    share_rows = down_rank.shape[1]
    inputs_part = lax.dynamic_slice_in_dim(normed_in, tensor_rank * share_rows, share_rows, 2)
    partial_rank = jnp.einsum(
        "sbd,pdr->sbpr", inputs_part, down_rank, preferred_element_type=jnp.float32
    )
    rank_sum = lax.psum(partial_rank, "tensor")
    lowrank_activity = rank_sum.astype(jnp.bfloat16)
    heads_here = frozen_query.shape[2] // HD
    query_correction = jnp.einsum(
        "huo,oa->hua",
        lowrank_activity[:, :, 0],
        query_up_columns,
        preferred_element_type=jnp.float32,
    )
    query_vectors = (frozen_query.astype(jnp.float32) + ADAPTER_SCALING * query_correction).astype(
        jnp.bfloat16
    )
    query_vectors = query_vectors.reshape(step_count, row_count, heads_here, HD)
    key_value_correction = jnp.einsum(
        "sbpr,prc->psbc", lowrank_activity[:, :, 1:], up_kv_full, preferred_element_type=jnp.float32
    )
    current_key_value = (
        frozen_key_value.astype(jnp.float32) + ADAPTER_SCALING * key_value_correction
    ).astype(jnp.bfloat16)
    current_key_value = current_key_value.reshape(2, step_count, row_count, KV, HD)
    head_ids = tensor_rank * heads_here + jnp.arange(heads_here)
    selector = (head_ids[:, None] // (HEADS // KV) == jnp.arange(KV)[None, :]).astype(jnp.bfloat16)
    fresh_heads = jnp.einsum(
        "psbgd,hg->psbhd", current_key_value, selector, preferred_element_type=jnp.float32
    ).astype(jnp.bfloat16)
    appended_keys = fresh_heads[0]
    appended_values = fresh_heads[1]
    slot_count = cache_keys.shape[2]
    cache_scores = jnp.einsum(
        "sbhd,bhpd->sbhp", query_vectors, cache_keys, preferred_element_type=jnp.float32
    ) / math.sqrt(HD)
    visible = jnp.arange(slot_count)[None, None, None, :] < lengths[None, :, None, None]
    cache_scores = jnp.where(visible, cache_scores, NEG_FILL)
    fresh_scores = jnp.einsum(
        "sbhd,tbhd->sbht", query_vectors, appended_keys, preferred_element_type=jnp.float32
    ) / math.sqrt(HD)
    causal = jnp.arange(step_count)[None, :] <= jnp.arange(step_count)[:, None]
    fresh_scores = jnp.where(causal[:, None, None, :], fresh_scores, NEG_FILL)
    highest = jnp.maximum(jnp.max(cache_scores, axis=-1), jnp.max(fresh_scores, axis=-1))[..., None]
    cache_exp = jnp.exp(cache_scores - highest)
    fresh_exp = jnp.exp(fresh_scores - highest)
    denominator = jnp.sum(cache_exp, axis=-1, keepdims=True) + jnp.sum(
        fresh_exp, axis=-1, keepdims=True
    )
    cache_weights = (cache_exp / denominator).astype(jnp.bfloat16)
    fresh_weights = (fresh_exp / denominator).astype(jnp.bfloat16)
    mixed = jnp.einsum(
        "sbhp,bhpd->sbhd", cache_weights, cache_values, preferred_element_type=jnp.float32
    )
    mixed = mixed + jnp.einsum(
        "sbht,tbhd->sbhd", fresh_weights, appended_values, preferred_element_type=jnp.float32
    )
    attention_result = mixed.astype(jnp.bfloat16).reshape(step_count, row_count, heads_here * HD)
    base_part = jnp.einsum(
        "sbc,cd->sbd", attention_result, out_weight, preferred_element_type=jnp.float32
    )
    lowrank_portion = jnp.einsum(
        "njk,ko->njo", attention_result, output_down_rows, preferred_element_type=jnp.float32
    )
    output_up_complete = lax.all_gather(up_o_cols, "tensor", axis=1, tiled=True)
    frozen_total_sum, lowrank_output = lax.psum((base_part, lowrank_portion), "tensor")
    widened_heads = jnp.einsum(
        "hwt,tm->hwm",
        lowrank_output,
        output_up_complete.astype(jnp.float32),
        precision=lax.Precision.HIGHEST,
    )
    refreshed_state = hidden_state + (frozen_total_sum + ADAPTER_SCALING * widened_heads)
    normed_out = (
        refreshed_state * rms_scale(refreshed_state) * norm_gain.astype(jnp.float32)
    ).astype(jnp.bfloat16)
    share_width = refreshed_state.shape[2] // tensor_count
    residual_out = lax.dynamic_slice_in_dim(
        refreshed_state, tensor_rank * share_width, share_width, 2
    ).astype(jnp.bfloat16)
    return (residual_out, normed_out)


BLOCK = 512
SLOTS = 8
MESH = pl.DeviceIdType.MESH


def fits(mesh):
    return KV % mesh.shape["tensor"] == 0


def dot_nt(a, b):
    return lax.dot_general(a, b, (((1,), (1,)), ((), ())), preferred_element_type=jnp.float32)


def fused_kernel(
    steps,
    replicas,
    shards,
    hid,
    frozen_q,
    frozen_kv,
    lens,
    up_q,
    up_kv,
    up_o,
    gain,
    down_hbm,
    down_o_hbm,
    keys_hbm,
    values_hbm,
    weight_hbm,
    res_out,
    norm_out,
    keys,
    values,
    wbuf,
    down,
    down_o,
    hid_all,
    up_q_all,
    up_kv_all,
    up_o_all,
    down_o_all,
    part,
    part_all,
    q_heads,
    k_heads,
    v_heads,
    att_heads,
    sums_out,
    sums_in,
    own,
    rank_out,
    full,
    kv_sem,
    w_sem,
    down_sem,
    rep_send,
    rep_recv,
    part_send,
    part_recv,
    sum_send,
    sum_recv,
    rank_send,
    rank_recv,
    full_send,
    full_recv,
):
    me_r = lax.axis_index("replica")
    me_t = lax.axis_index("tensor")
    tokens, width = hid.shape
    rows = tokens // steps
    share = width // shards
    chunks = share // BLOCK
    heads = keys.shape[1]
    slots = keys.shape[2]
    rank_share = up_q.shape[0]
    kv_width = up_kv_all.shape[3]
    depth = hid_all.shape[2]

    def key_copy(b):
        return pltpu.make_async_copy(keys_hbm.at[b], keys.at[b], kv_sem.at[0, b])

    def value_copy(b):
        return pltpu.make_async_copy(values_hbm.at[b], values.at[b], kv_sem.at[1, b])

    def weight_copy(m, c, slot):
        column = pl.multiple_of(lax.rem(me_t + m, shards) * share + c * BLOCK, BLOCK)
        return pltpu.make_async_copy(
            weight_hbm.at[:, pl.ds(column, BLOCK)], wbuf.at[slot], w_sem.at[slot]
        )

    down_copy = pltpu.make_async_copy(down_hbm, down, down_sem.at[0])
    down_o_copy = pltpu.make_async_copy(down_o_hbm, down_o, down_sem.at[1])
    down_copy.start()
    down_o_copy.start()

    @pl.loop(0, rows)
    def _(b):
        key_copy(b).start()
        value_copy(b).start()

    order = [m % shards for m in range(1, shards + 1)]
    held = SLOTS // chunks
    for place in range(min(held, shards)):

        @pl.loop(0, chunks)
        def _(c, place=place):
            weight_copy(order[place], c, place * chunks + c).start()

    barrier = pltpu.get_barrier_semaphore()
    for k in range(replicas):
        for m in range(shards):
            if k or m:
                pl.semaphore_signal(
                    barrier,
                    inc=1,
                    device_id={
                        "replica": lax.rem(me_r + k, replicas),
                        "tensor": lax.rem(me_t + m, shards),
                    },
                    device_id_type=MESH,
                )
    pl.semaphore_wait(barrier, replicas * shards - 1)

    def to_replica(src, dst, what, k):
        return pltpu.make_async_remote_copy(
            src_ref=src,
            dst_ref=dst.at[k],
            send_sem=rep_send.at[what, k],
            recv_sem=rep_recv.at[what, k],
            device_id={"replica": lax.rem(me_r + k, replicas)},
            device_id_type=MESH,
        )

    def to_shard(src, dst, send, recv, m):
        return pltpu.make_async_remote_copy(
            src_ref=src,
            dst_ref=dst,
            send_sem=send,
            recv_sem=recv,
            device_id={"tensor": lax.rem(me_t + m, shards)},
            device_id_type=MESH,
        )

    hid_mine = hid.at[:, pl.ds(pl.multiple_of(me_t * depth, 128), depth)]
    kv_mine = up_kv.at[:, :, pl.ds(pl.multiple_of(me_t * kv_width, 128), kv_width)]
    hid_copies = [to_replica(hid_mine, hid_all, 0, k) for k in range(1, replicas)]
    up_q_copies = [to_replica(up_q, up_q_all, 1, k) for k in range(1, replicas)]
    up_kv_copies = [to_replica(kv_mine, up_kv_all, 2, k) for k in range(1, replicas)]
    up_o_copies = [to_replica(up_o, up_o_all, 3, k) for k in range(1, replicas)]
    for copy in hid_copies + up_q_copies + up_kv_copies:
        copy.start()
    hid_all[0] = hid_mine[...]
    up_q_all[0] = up_q[...]
    up_kv_all[0] = kv_mine[...]
    up_o_all[0] = up_o[...]

    state = hid[...].astype(jnp.float32)
    scale = lax.rsqrt(jnp.mean(state * state, axis=-1, keepdims=True) + EPSILON)

    down_copy.wait()
    for copy in hid_copies:
        copy.wait_recv()
    hid_rows = hid_all[...].reshape(replicas * tokens, depth)
    pieces = [
        jnp.dot(hid_rows, down[p], preferred_element_type=jnp.float32) for p in range(3)
    ]
    pieces.append(jnp.zeros((replicas * tokens, 128 - 3 * rank_share), jnp.float32))
    part[...] = jnp.concatenate(pieces, axis=1).reshape(replicas, tokens, 128)
    part_copies = []
    for k in range(replicas):
        for m in range(shards):
            if k or m:
                back = (replicas - k) % replicas
                part_copies.append(
                    pltpu.make_async_remote_copy(
                        src_ref=part.at[k],
                        dst_ref=part_all.at[back, m],
                        send_sem=part_send.at[back, m],
                        recv_sem=part_recv.at[back, m],
                        device_id={
                            "replica": lax.rem(me_r + back, replicas),
                            "tensor": lax.rem(me_t + m, shards),
                        },
                        device_id_type=MESH,
                    )
                )
                part_copies[-1].start()
    part_all[0, 0] = part[0]

    down_o_copy.wait()
    eye = jnp.where(
        lax.broadcasted_iota(jnp.int32, (rank_share, rank_share), 0)
        == lax.broadcasted_iota(jnp.int32, (rank_share, rank_share), 1),
        1.0,
        0.0,
    ).astype(jnp.bfloat16)
    down_o_all[0] = dot_nt(eye, down_o[...]).astype(jnp.bfloat16)
    down_o_copies = [
        to_replica(down_o_all.at[0], down_o_all, 4, k) for k in range(1, replicas)
    ]
    for copy in down_o_copies + up_o_copies:
        copy.start()

    for copy in part_copies:
        copy.wait_recv()
    ranks = []
    for k in range(replicas):
        total = part_all[k, 0]
        for m in range(1, shards):
            total = total + part_all[k, m]
        ranks.append((total * scale).astype(jnp.bfloat16))

    def rank_of(p):
        return jnp.concatenate(
            [r[:, p * rank_share : (p + 1) * rank_share] for r in ranks], axis=1
        )

    for copy in up_q_copies + up_kv_copies:
        copy.wait_recv()
    queries = frozen_q[...].astype(jnp.float32) + ADAPTER_SCALING * jnp.dot(
        rank_of(0),
        up_q_all[...].reshape(replicas * rank_share, up_q.shape[1]),
        preferred_element_type=jnp.float32,
    )
    queries = queries.astype(jnp.bfloat16).astype(jnp.float32)
    for h in range(heads):
        q_heads[h] = queries[:, h * HD : (h + 1) * HD]
    group = HEADS // KV
    kv_columns = pl.ds(pl.multiple_of(me_t * kv_width, 128), kv_width)
    for p, target in ((0, k_heads), (1, v_heads)):
        up = jnp.concatenate([up_kv_all[k, p] for k in range(replicas)], axis=0)
        fresh = frozen_kv[p, :, kv_columns].astype(jnp.float32) + ADAPTER_SCALING * jnp.dot(
            rank_of(1 + p), up, preferred_element_type=jnp.float32
        )
        fresh = fresh.astype(jnp.bfloat16).astype(jnp.float32)
        for h in range(heads):
            g = h // group
            target[h] = fresh[:, g * HD : (g + 1) * HD]

    lines = steps * heads
    line_head = lax.rem(lax.broadcasted_iota(jnp.int32, (lines, HD), 0), heads)
    line_step = lax.broadcasted_iota(jnp.int32, (lines, 1), 0) // heads
    place = lax.broadcasted_iota(jnp.int32, (lines, slots), 1)
    root = 1.0 / math.sqrt(HD)

    @pl.loop(0, rows)
    def _(b):
        key_copy(b).wait()
        value_copy(b).wait()

        def line(source, s):
            return source[:, pl.ds(s * rows + b, 1), :].reshape(heads, HD)

        query = jnp.concatenate([line(q_heads, s) for s in range(steps)], axis=0)
        scores = jnp.zeros((lines, slots), jnp.float32)
        for h in range(0, heads, 2):
            left = jnp.concatenate(
                [jnp.where(line_head == h + i, query, 0.0) for i in range(2)], axis=1
            ).astype(jnp.bfloat16)
            pair = jnp.concatenate([keys[b, h], keys[b, h + 1]], axis=1)
            scores = scores + dot_nt(left, pair)
        scores = jnp.where(place < lens[b], scores * root, NEG_FILL)
        highest = jnp.max(scores, axis=-1, keepdims=True)
        fresh_scores = []
        for t in range(steps):
            new_key = jnp.concatenate([line(k_heads, t)] * steps, axis=0)
            score = jnp.sum(query * new_key, axis=-1, keepdims=True) * root
            score = jnp.where(line_step >= t, score, NEG_FILL)
            fresh_scores.append(score)
            highest = jnp.maximum(highest, score)
        weights = jnp.exp(scores - highest)
        total = jnp.sum(weights, axis=-1, keepdims=True)
        fresh_exp = [jnp.exp(score - highest) for score in fresh_scores]
        for value in fresh_exp:
            total = total + value
        inverse = 1.0 / total
        probs = (weights * inverse).astype(jnp.bfloat16)
        mixed = jnp.zeros((lines, HD), jnp.float32)
        for t in range(steps):
            new_value = jnp.concatenate([line(v_heads, t)] * steps, axis=0)
            prob = (fresh_exp[t] * inverse).astype(jnp.bfloat16).astype(jnp.float32)
            mixed = mixed + prob * new_value
        for h in range(0, heads, 2):
            pair = jnp.concatenate([values[b, h], values[b, h + 1]], axis=1)
            both = jnp.dot(probs, pair, preferred_element_type=jnp.float32)
            for i in range(2):
                mixed = mixed + jnp.where(
                    line_head == h + i, both[:, i * HD : (i + 1) * HD], 0.0
                )
        for s in range(steps):
            att_heads[:, pl.ds(s * rows + b, 1), :] = mixed[
                s * heads : (s + 1) * heads
            ].reshape(heads, 1, HD)

    attended = jnp.concatenate([att_heads[h] for h in range(heads)], axis=1).astype(jnp.bfloat16)

    for copy in down_o_copies:
        copy.wait_recv()
    low = dot_nt(attended, down_o_all[...].reshape(replicas * rank_share, depth))
    rank_total = replicas * rank_share
    rank_out[0] = jnp.concatenate(
        [low, jnp.zeros((tokens, 128 - rank_total), jnp.float32)], axis=1
    )
    rank_copies = [
        to_shard(rank_out.at[0], rank_out.at[m], rank_send.at[m], rank_recv.at[m], m)
        for m in range(1, shards)
    ]
    for copy in rank_copies:
        copy.start()

    def sum_copy(m, c):
        return to_shard(
            sums_out.at[m, c], sums_in.at[m, c], sum_send.at[m, c], sum_recv.at[m, c], m
        )

    for spot, m in enumerate(order):
        base = (spot % held) * chunks

        @pl.loop(0, chunks)
        def _(c, m=m, spot=spot, base=base):
            weight_copy(m, c, base + c).wait()
            product = jnp.dot(attended, wbuf[base + c], preferred_element_type=jnp.float32)
            if m:
                sums_out[m, c] = product.astype(jnp.bfloat16)
                sum_copy(m, c).start()
            else:
                own[c] = product
            if spot + held < shards:
                weight_copy(order[spot + held], c, base + c).start()

    for copy in rank_copies + up_o_copies:
        copy.wait_recv()
    rank_sum = rank_out[0]
    for m in range(1, shards):
        rank_sum = rank_sum + rank_out[m]
    rank_sum = rank_sum[:, :rank_total] * ADAPTER_SCALING
    rank_high = rank_sum.astype(jnp.bfloat16)
    rank_low = (rank_sum - rank_high.astype(jnp.float32)).astype(jnp.bfloat16)

    def full_copy(m, c):
        spot = me_t * chunks + c
        return to_shard(
            full.at[spot], full.at[spot], full_send.at[m, c], full_recv.at[m, c], m
        )

    for c in range(chunks):
        columns = slice(c * BLOCK, (c + 1) * BLOCK)
        up = jnp.concatenate([up_o_all[k, :, columns] for k in range(replicas)], axis=0)
        updated = jnp.dot(rank_high, up, preferred_element_type=jnp.float32) + jnp.dot(
            rank_low, up, preferred_element_type=jnp.float32
        )
        mine = pl.ds(pl.multiple_of(me_t * share + c * BLOCK, BLOCK), BLOCK)
        updated = updated + own[c] + hid[:, mine].astype(jnp.float32)
        for m in range(1, shards):
            sum_copy(m, c).wait_recv()
            updated = updated + sums_in[m, c].astype(jnp.float32)
        rounded = updated.astype(jnp.bfloat16)
        res_out[:, columns] = rounded
        full[me_t * chunks + c] = rounded
        for m in range(1, shards):
            full_copy(m, c).start()

    def arrived(m, c):
        spot = lax.rem(me_t + shards - m, shards) * chunks + c
        return to_shard(
            full.at[spot], full.at[spot], full_send.at[m, c], full_recv.at[m, c], m
        )

    for c in range(chunks):
        for m in range(1, shards):
            arrived(m, c).wait_recv()
    square = jnp.zeros((tokens, BLOCK), jnp.float32)
    for i in range(shards * chunks):
        block = full[i].astype(jnp.float32)
        square = square + block * block
    norm = lax.rsqrt(jnp.sum(square, axis=-1, keepdims=True) / width + EPSILON)
    for i in range(shards * chunks):
        columns = slice(i * BLOCK, (i + 1) * BLOCK)
        norm_out[:, columns] = (
            full[i].astype(jnp.float32) * norm * gain[:, columns].astype(jnp.float32)
        ).astype(jnp.bfloat16)

    for copy in (
        hid_copies + up_q_copies + up_kv_copies + up_o_copies + down_o_copies + part_copies
    ):
        copy.wait_send()
    for copy in rank_copies:
        copy.wait_send()
    for m in range(1, shards):
        for c in range(chunks):
            sum_copy(m, c).wait_send()
            full_copy(m, c).wait_send()


def body_fused(
    hidden,
    frozen_query,
    frozen_key_value,
    cache_keys,
    cache_values,
    lengths,
    out_weight,
    down_qkv,
    query_up_factor,
    key_value_up_factor,
    output_down_factor,
    output_up_factor,
    norm_gain,
):
    replicas = lax.axis_size("replica")
    shards = lax.axis_size("tensor")
    steps, rows, width = hidden.shape
    tokens = steps * rows
    share = width // shards
    chunks = share // BLOCK
    head_count = cache_keys.shape[1]
    depth = out_weight.shape[0]
    rank_share = query_up_factor.shape[0]
    kv_width = key_value_up_factor.shape[2] // shards
    vmem = pl.BlockSpec(memory_space=pltpu.VMEM)
    smem = pl.BlockSpec(memory_space=pltpu.SMEM)
    hbm = pl.BlockSpec(memory_space=pl.ANY)
    bf16, f32 = jnp.bfloat16, jnp.float32
    dma = pltpu.SemaphoreType.DMA
    per_head = pltpu.VMEM((head_count, tokens, HD), f32)
    residual, normed = pl.pallas_call(
        functools.partial(fused_kernel, steps, replicas, shards),
        out_shape=(
            jax.ShapeDtypeStruct((tokens, share), bf16),
            jax.ShapeDtypeStruct((tokens, width), bf16),
        ),
        in_specs=[vmem] * 3 + [smem] + [vmem] * 4 + [hbm] * 5,
        out_specs=(vmem, vmem),
        scratch_shapes=[
            pltpu.VMEM(cache_keys.shape, bf16),
            pltpu.VMEM(cache_values.shape, bf16),
            pltpu.VMEM((SLOTS, depth, BLOCK), bf16),
            pltpu.VMEM(down_qkv.shape, bf16),
            pltpu.VMEM(output_down_factor.shape, bf16),
            pltpu.VMEM((replicas, tokens, depth), bf16),
            pltpu.VMEM((replicas, rank_share, depth), bf16),
            pltpu.VMEM((replicas, 2, rank_share, kv_width), bf16),
            pltpu.VMEM((replicas, rank_share, share), bf16),
            pltpu.VMEM((replicas, rank_share, depth), bf16),
            pltpu.VMEM((replicas, tokens, 128), f32),
            pltpu.VMEM((replicas, shards, tokens, 128), f32),
            per_head,
            per_head,
            per_head,
            per_head,
            pltpu.VMEM((shards, chunks, tokens, BLOCK), bf16),
            pltpu.VMEM((shards, chunks, tokens, BLOCK), bf16),
            pltpu.VMEM((chunks, tokens, BLOCK), f32),
            pltpu.VMEM((shards, tokens, 128), f32),
            pltpu.VMEM((shards * chunks, tokens, BLOCK), bf16),
            dma((2, rows)),
            dma((SLOTS,)),
            dma((2,)),
            dma((5, replicas)),
            dma((5, replicas)),
            dma((replicas, shards)),
            dma((replicas, shards)),
            dma((shards, chunks)),
            dma((shards, chunks)),
            dma((shards,)),
            dma((shards,)),
            dma((shards, chunks)),
            dma((shards, chunks)),
        ],
        compiler_params=pltpu.CompilerParams(
            collective_id=0, has_side_effects=True, vmem_limit_bytes=62 * 2**20
        ),
    )(
        hidden.reshape(tokens, width),
        frozen_query.reshape(tokens, frozen_query.shape[2]),
        frozen_key_value.reshape(2, tokens, frozen_key_value.shape[3]),
        lengths,
        query_up_factor,
        key_value_up_factor,
        output_up_factor,
        norm_gain.reshape(1, width),
        down_qkv,
        output_down_factor,
        cache_keys,
        cache_values,
        out_weight,
    )
    return residual.reshape(steps, rows, share), normed.reshape(steps, rows, width)


def solution(mesh):
    in_specs = (
        P(None, ("groups", "replica"), None),
        P(None, ("groups", "replica"), "tensor"),
        P(None, None, ("groups", "replica"), None),
        P(("groups", "replica"), "tensor", None, None),
        P(("groups", "replica"), "tensor", None, None),
        P(("groups", "replica")),
        P("tensor", None),
        P("groups", "tensor", "replica"),
        P(("groups", "replica"), "tensor"),
        P(None, ("groups", "replica"), None),
        P(("groups", "tensor"), "replica"),
        P(("groups", "replica"), "tensor"),
        P(),
    )
    out_specs = (P(None, ("groups", "replica"), "tensor"), P(None, ("groups", "replica"), None))
    chosen = body_fused if fits(mesh) else body
    return jax.shard_map(chosen, mesh=mesh, in_specs=in_specs, out_specs=out_specs, check_vma=False)
```

```python
import functools
import math

import jax
import jax.numpy as jnp
from jax import lax
from jax.experimental import pallas as pl
from jax.experimental.pallas import tpu as pltpu
from jax.sharding import PartitionSpec as P

HEADS = 64
KV = 8
HD = 128


EPSILON = 1e-06
ADAPTER_SCALING = 0.25
NEG_FILL = -1e30


def rms_scale(values):
    return lax.rsqrt(jnp.mean(values * values, axis=-1, keepdims=True) + EPSILON)


def body(
    hidden,
    frozen_query,
    frozen_key_value,
    cache_keys,
    cache_values,
    lengths,
    out_weight,
    down_qkv,
    query_up_factor,
    key_value_up_factor,
    output_down_factor,
    output_up_factor,
    norm_gain,
):
    tensor_rank = lax.axis_index("tensor")
    tensor_count = lax.axis_size("tensor")
    step_count = hidden.shape[0]
    row_count = hidden.shape[1]
    down_rank, query_up_columns, up_kv_full, output_down_rows, up_o_cols = (
        lax.all_gather(down_qkv, "replica", axis=2, tiled=True),
        lax.all_gather(query_up_factor, "replica", axis=0, tiled=True),
        lax.all_gather(key_value_up_factor, "replica", axis=1, tiled=True),
        lax.all_gather(output_down_factor, "replica", axis=1, tiled=True),
        lax.all_gather(output_up_factor, "replica", axis=0, tiled=True),
    )
    hidden_state = hidden.astype(jnp.float32)
    normed_in = (hidden_state * rms_scale(hidden_state)).astype(jnp.bfloat16)
    share_rows = down_rank.shape[1]
    inputs_part = lax.dynamic_slice_in_dim(normed_in, tensor_rank * share_rows, share_rows, 2)
    partial_rank = jnp.einsum(
        "sbd,pdr->sbpr", inputs_part, down_rank, preferred_element_type=jnp.float32
    )
    rank_sum = lax.psum(partial_rank, "tensor")
    lowrank_activity = rank_sum.astype(jnp.bfloat16)
    heads_here = frozen_query.shape[2] // HD
    query_correction = jnp.einsum(
        "huo,oa->hua",
        lowrank_activity[:, :, 0],
        query_up_columns,
        preferred_element_type=jnp.float32,
    )
    query_vectors = (frozen_query.astype(jnp.float32) + ADAPTER_SCALING * query_correction).astype(
        jnp.bfloat16
    )
    query_vectors = query_vectors.reshape(step_count, row_count, heads_here, HD)
    key_value_correction = jnp.einsum(
        "sbpr,prc->psbc", lowrank_activity[:, :, 1:], up_kv_full, preferred_element_type=jnp.float32
    )
    current_key_value = (
        frozen_key_value.astype(jnp.float32) + ADAPTER_SCALING * key_value_correction
    ).astype(jnp.bfloat16)
    current_key_value = current_key_value.reshape(2, step_count, row_count, KV, HD)
    head_ids = tensor_rank * heads_here + jnp.arange(heads_here)
    selector = (head_ids[:, None] // (HEADS // KV) == jnp.arange(KV)[None, :]).astype(jnp.bfloat16)
    fresh_heads = jnp.einsum(
        "psbgd,hg->psbhd", current_key_value, selector, preferred_element_type=jnp.float32
    ).astype(jnp.bfloat16)
    appended_keys = fresh_heads[0]
    appended_values = fresh_heads[1]
    slot_count = cache_keys.shape[2]
    cache_scores = jnp.einsum(
        "sbhd,bhpd->sbhp", query_vectors, cache_keys, preferred_element_type=jnp.float32
    ) / math.sqrt(HD)
    visible = jnp.arange(slot_count)[None, None, None, :] < lengths[None, :, None, None]
    cache_scores = jnp.where(visible, cache_scores, NEG_FILL)
    fresh_scores = jnp.einsum(
        "sbhd,tbhd->sbht", query_vectors, appended_keys, preferred_element_type=jnp.float32
    ) / math.sqrt(HD)
    causal = jnp.arange(step_count)[None, :] <= jnp.arange(step_count)[:, None]
    fresh_scores = jnp.where(causal[:, None, None, :], fresh_scores, NEG_FILL)
    highest = jnp.maximum(jnp.max(cache_scores, axis=-1), jnp.max(fresh_scores, axis=-1))[..., None]
    cache_exp = jnp.exp(cache_scores - highest)
    fresh_exp = jnp.exp(fresh_scores - highest)
    denominator = jnp.sum(cache_exp, axis=-1, keepdims=True) + jnp.sum(
        fresh_exp, axis=-1, keepdims=True
    )
    cache_weights = (cache_exp / denominator).astype(jnp.bfloat16)
    fresh_weights = (fresh_exp / denominator).astype(jnp.bfloat16)
    mixed = jnp.einsum(
        "sbhp,bhpd->sbhd", cache_weights, cache_values, preferred_element_type=jnp.float32
    )
    mixed = mixed + jnp.einsum(
        "sbht,tbhd->sbhd", fresh_weights, appended_values, preferred_element_type=jnp.float32
    )
    attention_result = mixed.astype(jnp.bfloat16).reshape(step_count, row_count, heads_here * HD)
    base_part = jnp.einsum(
        "sbc,cd->sbd", attention_result, out_weight, preferred_element_type=jnp.float32
    )
    lowrank_portion = jnp.einsum(
        "njk,ko->njo", attention_result, output_down_rows, preferred_element_type=jnp.float32
    )
    output_up_complete = lax.all_gather(up_o_cols, "tensor", axis=1, tiled=True)
    frozen_total_sum, lowrank_output = lax.psum((base_part, lowrank_portion), "tensor")
    widened_heads = jnp.einsum(
        "hwt,tm->hwm",
        lowrank_output,
        output_up_complete.astype(jnp.float32),
        precision=lax.Precision.HIGHEST,
    )
    refreshed_state = hidden_state + (frozen_total_sum + ADAPTER_SCALING * widened_heads)
    normed_out = (
        refreshed_state * rms_scale(refreshed_state) * norm_gain.astype(jnp.float32)
    ).astype(jnp.bfloat16)
    share_width = refreshed_state.shape[2] // tensor_count
    residual_out = lax.dynamic_slice_in_dim(
        refreshed_state, tensor_rank * share_width, share_width, 2
    ).astype(jnp.bfloat16)
    return (residual_out, normed_out)


BLOCK = 512
SLOTS = 8
MESH = pl.DeviceIdType.MESH


def fits(mesh):
    return KV % mesh.shape["tensor"] == 0


def dot_nt(a, b):
    return lax.dot_general(a, b, (((1,), (1,)), ((), ())), preferred_element_type=jnp.float32)


def fused_kernel(
    steps,
    replicas,
    shards,
    hid,
    frozen_q,
    frozen_kv,
    lens,
    up_q,
    up_kv,
    up_o,
    down_hbm,
    down_o_hbm,
    keys_hbm,
    values_hbm,
    weight_hbm,
    full,
    keys,
    values,
    wbuf,
    down,
    down_o,
    hid_all,
    up_q_all,
    up_kv_all,
    up_o_all,
    down_o_all,
    part,
    part_all,
    q_heads,
    k_heads,
    v_heads,
    att_heads,
    sums_out,
    sums_in,
    own,
    rank_out,
    kv_sem,
    w_sem,
    down_sem,
    rep_send,
    rep_recv,
    part_send,
    part_recv,
    sum_send,
    sum_recv,
    rank_send,
    rank_recv,
    full_send,
    full_recv,
):
    me_r = lax.axis_index("replica")
    me_t = lax.axis_index("tensor")
    tokens, width = hid.shape
    rows = tokens // steps
    share = width // shards
    chunks = share // BLOCK
    heads = keys.shape[1]
    slots = keys.shape[2]
    rank_share = up_q.shape[0]
    kv_width = up_kv_all.shape[3]
    depth = hid_all.shape[2]

    def key_copy(b):
        return pltpu.make_async_copy(keys_hbm.at[b], keys.at[b], kv_sem.at[0, b])

    def value_copy(b):
        return pltpu.make_async_copy(values_hbm.at[b], values.at[b], kv_sem.at[1, b])

    def weight_copy(m, c, slot):
        column = pl.multiple_of(lax.rem(me_t + m, shards) * share + c * BLOCK, BLOCK)
        return pltpu.make_async_copy(
            weight_hbm.at[:, pl.ds(column, BLOCK)], wbuf.at[slot], w_sem.at[slot]
        )

    down_copy = pltpu.make_async_copy(down_hbm, down, down_sem.at[0])
    down_o_copy = pltpu.make_async_copy(down_o_hbm, down_o, down_sem.at[1])
    down_copy.start()
    down_o_copy.start()

    @pl.loop(0, rows)
    def _(b):
        key_copy(b).start()
        value_copy(b).start()

    order = [m % shards for m in range(1, shards + 1)]
    held = SLOTS // chunks
    for place in range(min(held, shards)):

        @pl.loop(0, chunks)
        def _(c, place=place):
            weight_copy(order[place], c, place * chunks + c).start()

    barrier = pltpu.get_barrier_semaphore()
    for k in range(replicas):
        for m in range(shards):
            if k or m:
                pl.semaphore_signal(
                    barrier,
                    inc=1,
                    device_id={
                        "replica": lax.rem(me_r + k, replicas),
                        "tensor": lax.rem(me_t + m, shards),
                    },
                    device_id_type=MESH,
                )
    pl.semaphore_wait(barrier, replicas * shards - 1)

    def to_replica(src, dst, what, k):
        return pltpu.make_async_remote_copy(
            src_ref=src,
            dst_ref=dst.at[k],
            send_sem=rep_send.at[what, k],
            recv_sem=rep_recv.at[what, k],
            device_id={"replica": lax.rem(me_r + k, replicas)},
            device_id_type=MESH,
        )

    def to_shard(src, dst, send, recv, m):
        return pltpu.make_async_remote_copy(
            src_ref=src,
            dst_ref=dst,
            send_sem=send,
            recv_sem=recv,
            device_id={"tensor": lax.rem(me_t + m, shards)},
            device_id_type=MESH,
        )

    state = hid[...].astype(jnp.float32)
    scale = lax.rsqrt(jnp.mean(state * state, axis=-1, keepdims=True) + EPSILON)
    hid_mine = hid[:, pl.ds(pl.multiple_of(me_t * depth, 128), depth)].astype(jnp.float32)
    hid_all[0] = (hid_mine * scale).astype(jnp.bfloat16)
    kv_mine = up_kv.at[:, :, pl.ds(pl.multiple_of(me_t * kv_width, 128), kv_width)]
    hid_copies = [to_replica(hid_all.at[0], hid_all, 0, k) for k in range(1, replicas)]
    up_q_copies = [to_replica(up_q, up_q_all, 1, k) for k in range(1, replicas)]
    up_kv_copies = [to_replica(kv_mine, up_kv_all, 2, k) for k in range(1, replicas)]
    up_o_copies = [to_replica(up_o, up_o_all, 3, k) for k in range(1, replicas)]
    for copy in hid_copies + up_q_copies + up_kv_copies:
        copy.start()
    up_q_all[0] = up_q[...]
    up_kv_all[0] = kv_mine[...]
    up_o_all[0] = up_o[...]

    down_copy.wait()
    for copy in hid_copies:
        copy.wait_recv()
    hid_rows = hid_all[...].reshape(replicas * tokens, depth)
    partial = dot_nt(hid_rows, down[...].reshape(3 * rank_share, depth))
    blank = jnp.zeros((replicas * tokens, 128 - 3 * rank_share), jnp.float32)
    part[...] = jnp.concatenate([partial, blank], axis=1).reshape(replicas, tokens, 128)
    part_copies = []
    for k in range(replicas):
        for m in range(shards):
            if k or m:
                back = (replicas - k) % replicas
                part_copies.append(
                    pltpu.make_async_remote_copy(
                        src_ref=part.at[k],
                        dst_ref=part_all.at[back, m],
                        send_sem=part_send.at[back, m],
                        recv_sem=part_recv.at[back, m],
                        device_id={
                            "replica": lax.rem(me_r + back, replicas),
                            "tensor": lax.rem(me_t + m, shards),
                        },
                        device_id_type=MESH,
                    )
                )
                part_copies[-1].start()
    part_all[0, 0] = part[0]

    down_o_copy.wait()
    down_o_all[0] = down_o[...]
    down_o_copies = [to_replica(down_o, down_o_all, 4, k) for k in range(1, replicas)]
    for copy in down_o_copies + up_o_copies:
        copy.start()

    for copy in part_copies:
        copy.wait_recv()
    ranks = []
    for k in range(replicas):
        total = part_all[k, 0]
        for m in range(1, shards):
            total = total + part_all[k, m]
        ranks.append(total.astype(jnp.bfloat16))

    def rank_of(p):
        return jnp.concatenate(
            [r[:, p * rank_share : (p + 1) * rank_share] for r in ranks], axis=1
        )

    for copy in up_q_copies + up_kv_copies:
        copy.wait_recv()
    queries = frozen_q[...].astype(jnp.float32) + ADAPTER_SCALING * jnp.dot(
        rank_of(0),
        up_q_all[...].reshape(replicas * rank_share, up_q.shape[1]),
        preferred_element_type=jnp.float32,
    )
    queries = queries.astype(jnp.bfloat16).astype(jnp.float32)
    for h in range(heads):
        q_heads[h] = queries[:, h * HD : (h + 1) * HD]
    group = HEADS // KV
    kv_columns = pl.ds(pl.multiple_of(me_t * kv_width, 128), kv_width)
    for p, target in ((0, k_heads), (1, v_heads)):
        up = jnp.concatenate([up_kv_all[k, p] for k in range(replicas)], axis=0)
        fresh = frozen_kv[p, :, kv_columns].astype(jnp.float32) + ADAPTER_SCALING * jnp.dot(
            rank_of(1 + p), up, preferred_element_type=jnp.float32
        )
        fresh = fresh.astype(jnp.bfloat16).astype(jnp.float32)
        for h in range(heads):
            g = h // group
            target[h] = fresh[:, g * HD : (g + 1) * HD]

    lines = steps * heads
    line_head = lax.rem(lax.broadcasted_iota(jnp.int32, (lines, HD), 0), heads)
    line_step = lax.broadcasted_iota(jnp.int32, (lines, 1), 0) // heads
    place = lax.broadcasted_iota(jnp.int32, (lines, slots), 1)
    root = 1.0 / math.sqrt(HD)

    @pl.loop(0, rows)
    def _(b):
        key_copy(b).wait()
        value_copy(b).wait()

        def line(source, s):
            return source[:, pl.ds(s * rows + b, 1), :].reshape(heads, HD)

        query = jnp.concatenate([line(q_heads, s) for s in range(steps)], axis=0)
        scores = jnp.zeros((lines, slots), jnp.float32)
        for h in range(0, heads, 2):
            left = jnp.concatenate(
                [jnp.where(line_head == h + i, query, 0.0) for i in range(2)], axis=1
            ).astype(jnp.bfloat16)
            pair = jnp.concatenate([keys[b, h], keys[b, h + 1]], axis=1)
            scores = scores + dot_nt(left, pair)
        scores = jnp.where(place < lens[b], scores * root, NEG_FILL)
        highest = jnp.max(scores, axis=-1, keepdims=True)
        fresh_scores = []
        for t in range(steps):
            new_key = jnp.concatenate([line(k_heads, t)] * steps, axis=0)
            score = jnp.sum(query * new_key, axis=-1, keepdims=True) * root
            score = jnp.where(line_step >= t, score, NEG_FILL)
            fresh_scores.append(score)
            highest = jnp.maximum(highest, score)
        weights = jnp.exp(scores - highest)
        total = jnp.sum(weights, axis=-1, keepdims=True)
        fresh_exp = [jnp.exp(score - highest) for score in fresh_scores]
        for value in fresh_exp:
            total = total + value
        inverse = 1.0 / total
        probs = (weights * inverse).astype(jnp.bfloat16)
        mixed = jnp.zeros((lines, HD), jnp.float32)
        for t in range(steps):
            new_value = jnp.concatenate([line(v_heads, t)] * steps, axis=0)
            prob = (fresh_exp[t] * inverse).astype(jnp.bfloat16).astype(jnp.float32)
            mixed = mixed + prob * new_value
        for h in range(0, heads, 2):
            pair = jnp.concatenate([values[b, h], values[b, h + 1]], axis=1)
            both = jnp.dot(probs, pair, preferred_element_type=jnp.float32)
            for i in range(2):
                mixed = mixed + jnp.where(
                    line_head == h + i, both[:, i * HD : (i + 1) * HD], 0.0
                )
        for s in range(steps):
            att_heads[:, pl.ds(s * rows + b, 1), :] = mixed[
                s * heads : (s + 1) * heads
            ].reshape(heads, 1, HD)

    attended = jnp.concatenate([att_heads[h] for h in range(heads)], axis=1).astype(jnp.bfloat16)

    for copy in down_o_copies:
        copy.wait_recv()
    low = dot_nt(attended, down_o_all[...].reshape(replicas * rank_share, depth))
    rank_total = replicas * rank_share
    rank_out[0] = jnp.concatenate(
        [low, jnp.zeros((tokens, 128 - rank_total), jnp.float32)], axis=1
    )
    rank_copies = [
        to_shard(rank_out.at[0], rank_out.at[m], rank_send.at[m], rank_recv.at[m], m)
        for m in range(1, shards)
    ]
    for copy in rank_copies:
        copy.start()

    def sum_copy(m, c):
        return to_shard(
            sums_out.at[m, c], sums_in.at[m, c], sum_send.at[m, c], sum_recv.at[m, c], m
        )

    for spot, m in enumerate(order):
        base = (spot % held) * chunks

        @pl.loop(0, chunks)
        def _(c, m=m, spot=spot, base=base):
            weight_copy(m, c, base + c).wait()
            product = jnp.dot(attended, wbuf[base + c], preferred_element_type=jnp.float32)
            if m:
                sums_out[m, c] = product.astype(jnp.bfloat16)
                sum_copy(m, c).start()
            else:
                own[c] = product
            if spot + held < shards:
                weight_copy(order[spot + held], c, base + c).start()

    for copy in rank_copies + up_o_copies:
        copy.wait_recv()
    rank_sum = rank_out[0]
    for m in range(1, shards):
        rank_sum = rank_sum + rank_out[m]
    rank_sum = rank_sum[:, :rank_total] * ADAPTER_SCALING
    rank_high = rank_sum.astype(jnp.bfloat16)
    rank_low = (rank_sum - rank_high.astype(jnp.float32)).astype(jnp.bfloat16)

    def full_copy(m, c):
        spot = me_t * chunks + c
        return to_shard(
            full.at[spot], full.at[spot], full_send.at[m, c], full_recv.at[m, c], m
        )

    for c in range(chunks):
        columns = slice(c * BLOCK, (c + 1) * BLOCK)
        up = jnp.concatenate([up_o_all[k, :, columns] for k in range(replicas)], axis=0)
        updated = jnp.dot(rank_high, up, preferred_element_type=jnp.float32) + jnp.dot(
            rank_low, up, preferred_element_type=jnp.float32
        )
        mine = pl.ds(pl.multiple_of(me_t * share + c * BLOCK, BLOCK), BLOCK)
        updated = updated + own[c] + hid[:, mine].astype(jnp.float32)
        for m in range(1, shards):
            sum_copy(m, c).wait_recv()
            updated = updated + sums_in[m, c].astype(jnp.float32)
        rounded = updated.astype(jnp.bfloat16)
        full[me_t * chunks + c] = rounded
        for m in range(1, shards):
            full_copy(m, c).start()

    def arrived(m, c):
        spot = lax.rem(me_t + shards - m, shards) * chunks + c
        return to_shard(
            full.at[spot], full.at[spot], full_send.at[m, c], full_recv.at[m, c], m
        )

    for c in range(chunks):
        for m in range(1, shards):
            arrived(m, c).wait_recv()

    for copy in (
        hid_copies + up_q_copies + up_kv_copies + up_o_copies + down_o_copies + part_copies
    ):
        copy.wait_send()
    for copy in rank_copies:
        copy.wait_send()
    for m in range(1, shards):
        for c in range(chunks):
            sum_copy(m, c).wait_send()
            full_copy(m, c).wait_send()


def norm_kernel(full, gain, res_out, norm_out):
    blocks, tokens, block_width = full.shape
    chunks = res_out.shape[1] // block_width
    first = lax.axis_index("tensor") * chunks
    for c in range(chunks):
        res_out[:, c * block_width : (c + 1) * block_width] = full[first + c]
    square = jnp.zeros((tokens, block_width), jnp.float32)
    for i in range(blocks):
        block = full[i].astype(jnp.float32)
        square = square + block * block
    mean = jnp.sum(square, axis=-1, keepdims=True) / (blocks * block_width)
    norm = lax.rsqrt(mean + EPSILON)
    gains = gain[...].astype(jnp.float32)
    for i in range(blocks):
        block = full[i].astype(jnp.float32) * norm
        for j in range(0, block_width, 128):
            line = (i * block_width + j) // 128
            norm_out[:, i * block_width + j : i * block_width + j + 128] = (
                block[:, j : j + 128] * gains[line : line + 1]
            ).astype(jnp.bfloat16)


def body_fused(
    hidden,
    frozen_query,
    frozen_key_value,
    cache_keys,
    cache_values,
    lengths,
    out_weight,
    down_qkv,
    query_up_factor,
    key_value_up_factor,
    output_down_factor,
    output_up_factor,
    norm_gain,
):
    replicas = lax.axis_size("replica")
    shards = lax.axis_size("tensor")
    steps, rows, width = hidden.shape
    tokens = steps * rows
    share = width // shards
    chunks = share // BLOCK
    head_count = cache_keys.shape[1]
    depth = out_weight.shape[0]
    rank_share = query_up_factor.shape[0]
    kv_width = key_value_up_factor.shape[2] // shards
    vmem = pl.BlockSpec(memory_space=pltpu.VMEM)
    smem = pl.BlockSpec(memory_space=pltpu.SMEM)
    hbm = pl.BlockSpec(memory_space=pl.ANY)
    bf16, f32 = jnp.bfloat16, jnp.float32
    dma = pltpu.SemaphoreType.DMA
    per_head = pltpu.VMEM((head_count, tokens, HD), f32)
    down_qkv = jnp.swapaxes(down_qkv, 1, 2)
    output_down_factor = output_down_factor.T
    full = pl.pallas_call(
        functools.partial(fused_kernel, steps, replicas, shards),
        out_shape=jax.ShapeDtypeStruct((shards * chunks, tokens, BLOCK), bf16),
        in_specs=[vmem] * 3 + [smem] + [vmem] * 3 + [hbm] * 5,
        out_specs=vmem,
        scratch_shapes=[
            pltpu.VMEM(cache_keys.shape, bf16),
            pltpu.VMEM(cache_values.shape, bf16),
            pltpu.VMEM((SLOTS, depth, BLOCK), bf16),
            pltpu.VMEM(down_qkv.shape, bf16),
            pltpu.VMEM(output_down_factor.shape, bf16),
            pltpu.VMEM((replicas, tokens, depth), bf16),
            pltpu.VMEM((replicas, rank_share, depth), bf16),
            pltpu.VMEM((replicas, 2, rank_share, kv_width), bf16),
            pltpu.VMEM((replicas, rank_share, share), bf16),
            pltpu.VMEM((replicas, rank_share, depth), bf16),
            pltpu.VMEM((replicas, tokens, 128), f32),
            pltpu.VMEM((replicas, shards, tokens, 128), f32),
            per_head,
            per_head,
            per_head,
            per_head,
            pltpu.VMEM((shards, chunks, tokens, BLOCK), bf16),
            pltpu.VMEM((shards, chunks, tokens, BLOCK), bf16),
            pltpu.VMEM((chunks, tokens, BLOCK), f32),
            pltpu.VMEM((shards, tokens, 128), f32),
            dma((2, rows)),
            dma((SLOTS,)),
            dma((2,)),
            dma((5, replicas)),
            dma((5, replicas)),
            dma((replicas, shards)),
            dma((replicas, shards)),
            dma((shards, chunks)),
            dma((shards, chunks)),
            dma((shards,)),
            dma((shards,)),
            dma((shards, chunks)),
            dma((shards, chunks)),
        ],
        compiler_params=pltpu.CompilerParams(
            collective_id=0, has_side_effects=True, vmem_limit_bytes=62 * 2**20
        ),
    )(
        hidden.reshape(tokens, width),
        frozen_query.reshape(tokens, frozen_query.shape[2]),
        frozen_key_value.reshape(2, tokens, frozen_key_value.shape[3]),
        lengths,
        query_up_factor,
        key_value_up_factor,
        output_up_factor,
        down_qkv,
        output_down_factor,
        cache_keys,
        cache_values,
        out_weight,
    )
    residual, normed = pl.pallas_call(
        norm_kernel,
        out_shape=(
            jax.ShapeDtypeStruct((tokens, share), bf16),
            jax.ShapeDtypeStruct((tokens, width), bf16),
        ),
        in_specs=[vmem, vmem],
        out_specs=(vmem, vmem),
    )(full, norm_gain.reshape(width // 128, 128))
    return residual.reshape(steps, rows, share), normed.reshape(steps, rows, width)


def solution(mesh):
    in_specs = (
        P(None, ("groups", "replica"), None),
        P(None, ("groups", "replica"), "tensor"),
        P(None, None, ("groups", "replica"), None),
        P(("groups", "replica"), "tensor", None, None),
        P(("groups", "replica"), "tensor", None, None),
        P(("groups", "replica")),
        P("tensor", None),
        P("groups", "tensor", "replica"),
        P(("groups", "replica"), "tensor"),
        P(None, ("groups", "replica"), None),
        P(("groups", "tensor"), "replica"),
        P(("groups", "replica"), "tensor"),
        P(),
    )
    out_specs = (P(None, ("groups", "replica"), "tensor"), P(None, ("groups", "replica"), None))
    chosen = body_fused if fits(mesh) else body
    return jax.shard_map(chosen, mesh=mesh, in_specs=in_specs, out_specs=out_specs, check_vma=False)
```

```python
import functools
import math

import jax
import jax.numpy as jnp
from jax import lax
from jax.experimental import pallas as pl
from jax.experimental.pallas import tpu as pltpu
from jax.sharding import PartitionSpec as P

HEADS = 64
KV = 8
HD = 128


EPSILON = 1e-06
ADAPTER_SCALING = 0.25
NEG_FILL = -1e30


def rms_scale(values):
    return lax.rsqrt(jnp.mean(values * values, axis=-1, keepdims=True) + EPSILON)


def body(
    hidden,
    frozen_query,
    frozen_key_value,
    cache_keys,
    cache_values,
    lengths,
    out_weight,
    down_qkv,
    query_up_factor,
    key_value_up_factor,
    output_down_factor,
    output_up_factor,
    norm_gain,
):
    tensor_rank = lax.axis_index("tensor")
    tensor_count = lax.axis_size("tensor")
    step_count = hidden.shape[0]
    row_count = hidden.shape[1]
    down_rank, query_up_columns, up_kv_full, output_down_rows, up_o_cols = (
        lax.all_gather(down_qkv, "replica", axis=2, tiled=True),
        lax.all_gather(query_up_factor, "replica", axis=0, tiled=True),
        lax.all_gather(key_value_up_factor, "replica", axis=1, tiled=True),
        lax.all_gather(output_down_factor, "replica", axis=1, tiled=True),
        lax.all_gather(output_up_factor, "replica", axis=0, tiled=True),
    )
    hidden_state = hidden.astype(jnp.float32)
    normed_in = (hidden_state * rms_scale(hidden_state)).astype(jnp.bfloat16)
    share_rows = down_rank.shape[1]
    inputs_part = lax.dynamic_slice_in_dim(normed_in, tensor_rank * share_rows, share_rows, 2)
    partial_rank = jnp.einsum(
        "sbd,pdr->sbpr", inputs_part, down_rank, preferred_element_type=jnp.float32
    )
    rank_sum = lax.psum(partial_rank, "tensor")
    lowrank_activity = rank_sum.astype(jnp.bfloat16)
    heads_here = frozen_query.shape[2] // HD
    query_correction = jnp.einsum(
        "huo,oa->hua",
        lowrank_activity[:, :, 0],
        query_up_columns,
        preferred_element_type=jnp.float32,
    )
    query_vectors = (frozen_query.astype(jnp.float32) + ADAPTER_SCALING * query_correction).astype(
        jnp.bfloat16
    )
    query_vectors = query_vectors.reshape(step_count, row_count, heads_here, HD)
    key_value_correction = jnp.einsum(
        "sbpr,prc->psbc", lowrank_activity[:, :, 1:], up_kv_full, preferred_element_type=jnp.float32
    )
    current_key_value = (
        frozen_key_value.astype(jnp.float32) + ADAPTER_SCALING * key_value_correction
    ).astype(jnp.bfloat16)
    current_key_value = current_key_value.reshape(2, step_count, row_count, KV, HD)
    head_ids = tensor_rank * heads_here + jnp.arange(heads_here)
    selector = (head_ids[:, None] // (HEADS // KV) == jnp.arange(KV)[None, :]).astype(jnp.bfloat16)
    fresh_heads = jnp.einsum(
        "psbgd,hg->psbhd", current_key_value, selector, preferred_element_type=jnp.float32
    ).astype(jnp.bfloat16)
    appended_keys = fresh_heads[0]
    appended_values = fresh_heads[1]
    slot_count = cache_keys.shape[2]
    cache_scores = jnp.einsum(
        "sbhd,bhpd->sbhp", query_vectors, cache_keys, preferred_element_type=jnp.float32
    ) / math.sqrt(HD)
    visible = jnp.arange(slot_count)[None, None, None, :] < lengths[None, :, None, None]
    cache_scores = jnp.where(visible, cache_scores, NEG_FILL)
    fresh_scores = jnp.einsum(
        "sbhd,tbhd->sbht", query_vectors, appended_keys, preferred_element_type=jnp.float32
    ) / math.sqrt(HD)
    causal = jnp.arange(step_count)[None, :] <= jnp.arange(step_count)[:, None]
    fresh_scores = jnp.where(causal[:, None, None, :], fresh_scores, NEG_FILL)
    highest = jnp.maximum(jnp.max(cache_scores, axis=-1), jnp.max(fresh_scores, axis=-1))[..., None]
    cache_exp = jnp.exp(cache_scores - highest)
    fresh_exp = jnp.exp(fresh_scores - highest)
    denominator = jnp.sum(cache_exp, axis=-1, keepdims=True) + jnp.sum(
        fresh_exp, axis=-1, keepdims=True
    )
    cache_weights = (cache_exp / denominator).astype(jnp.bfloat16)
    fresh_weights = (fresh_exp / denominator).astype(jnp.bfloat16)
    mixed = jnp.einsum(
        "sbhp,bhpd->sbhd", cache_weights, cache_values, preferred_element_type=jnp.float32
    )
    mixed = mixed + jnp.einsum(
        "sbht,tbhd->sbhd", fresh_weights, appended_values, preferred_element_type=jnp.float32
    )
    attention_result = mixed.astype(jnp.bfloat16).reshape(step_count, row_count, heads_here * HD)
    base_part = jnp.einsum(
        "sbc,cd->sbd", attention_result, out_weight, preferred_element_type=jnp.float32
    )
    lowrank_portion = jnp.einsum(
        "njk,ko->njo", attention_result, output_down_rows, preferred_element_type=jnp.float32
    )
    output_up_complete = lax.all_gather(up_o_cols, "tensor", axis=1, tiled=True)
    frozen_total_sum, lowrank_output = lax.psum((base_part, lowrank_portion), "tensor")
    widened_heads = jnp.einsum(
        "hwt,tm->hwm",
        lowrank_output,
        output_up_complete.astype(jnp.float32),
        precision=lax.Precision.HIGHEST,
    )
    refreshed_state = hidden_state + (frozen_total_sum + ADAPTER_SCALING * widened_heads)
    normed_out = (
        refreshed_state * rms_scale(refreshed_state) * norm_gain.astype(jnp.float32)
    ).astype(jnp.bfloat16)
    share_width = refreshed_state.shape[2] // tensor_count
    residual_out = lax.dynamic_slice_in_dim(
        refreshed_state, tensor_rank * share_width, share_width, 2
    ).astype(jnp.bfloat16)
    return (residual_out, normed_out)


BLOCK = 1024
SLOTS = 4
ROWS = 4
MESH = pl.DeviceIdType.MESH


def fits(mesh):
    return KV % mesh.shape["tensor"] == 0


def dot_nt(a, b):
    return lax.dot_general(a, b, (((1,), (1,)), ((), ())), preferred_element_type=jnp.float32)


def fused_kernel(
    steps,
    replicas,
    shards,
    hid,
    frozen_q,
    frozen_kv,
    lens,
    up_q,
    up_kv,
    up_o,
    down_hbm,
    down_o_hbm,
    keys_hbm,
    values_hbm,
    weight_hbm,
    full,
    keys,
    values,
    wbuf,
    down,
    down_o,
    hid_all,
    up_q_all,
    up_kv_all,
    up_o_all,
    down_o_all,
    part,
    part_all,
    q_heads,
    k_heads,
    v_heads,
    att_heads,
    sums_out,
    sums_in,
    own,
    rank_out,
    kv_sem,
    w_sem,
    down_sem,
    rep_send,
    rep_recv,
    part_send,
    part_recv,
    sum_send,
    sum_recv,
    rank_send,
    rank_recv,
    full_send,
    full_recv,
):
    me_r = lax.axis_index("replica")
    me_t = lax.axis_index("tensor")
    tokens, width = hid.shape
    rows = tokens // steps
    share = width // shards
    chunks = share // BLOCK
    heads = keys.shape[1]
    slots = keys.shape[2]
    rank_share = up_q.shape[0]
    kv_width = up_kv_all.shape[3]
    depth = hid_all.shape[2]

    barrier = pltpu.get_barrier_semaphore()
    for k in range(replicas):
        for m in range(shards):
            if k or m:
                pl.semaphore_signal(
                    barrier,
                    inc=1,
                    device_id={
                        "replica": lax.rem(me_r + k, replicas),
                        "tensor": lax.rem(me_t + m, shards),
                    },
                    device_id_type=MESH,
                )
    def key_copy(b):
        return pltpu.make_async_copy(keys_hbm.at[b], keys.at[b], kv_sem.at[0, b])

    def value_copy(b):
        return pltpu.make_async_copy(values_hbm.at[b], values.at[b], kv_sem.at[1, b])

    def weight_copy(m, c, slot):
        column = pl.multiple_of(lax.rem(me_t + m, shards) * share + c * BLOCK, BLOCK)
        return pltpu.make_async_copy(
            weight_hbm.at[:, pl.ds(column, BLOCK)], wbuf.at[slot], w_sem.at[slot]
        )

    down_copy = pltpu.make_async_copy(down_hbm, down, down_sem.at[0])
    down_o_copy = pltpu.make_async_copy(down_o_hbm, down_o, down_sem.at[1])
    down_copy.start()
    down_o_copy.start()

    @pl.loop(0, rows)
    def _(b):
        key_copy(b).start()
        value_copy(b).start()

    order = [m % shards for m in range(1, shards + 1)]
    held = SLOTS // chunks
    for place in range(min(held, shards)):

        @pl.loop(0, chunks)
        def _(c, place=place):
            weight_copy(order[place], c, place * chunks + c).start()

    state = hid[...].astype(jnp.float32)
    scale = lax.rsqrt(jnp.mean(state * state, axis=-1, keepdims=True) + EPSILON)
    hid_mine = hid[:, pl.ds(pl.multiple_of(me_t * depth, 128), depth)].astype(jnp.float32)
    hid_all[0] = (hid_mine * scale).astype(jnp.bfloat16)
    pl.semaphore_wait(barrier, replicas * shards - 1)

    def to_replica(src, dst, what, k):
        return pltpu.make_async_remote_copy(
            src_ref=src,
            dst_ref=dst.at[k],
            send_sem=rep_send.at[what, k],
            recv_sem=rep_recv.at[what, k],
            device_id={"replica": lax.rem(me_r + k, replicas)},
            device_id_type=MESH,
        )

    def to_shard(src, dst, send, recv, m):
        return pltpu.make_async_remote_copy(
            src_ref=src,
            dst_ref=dst,
            send_sem=send,
            recv_sem=recv,
            device_id={"tensor": lax.rem(me_t + m, shards)},
            device_id_type=MESH,
        )

    kv_mine = up_kv.at[:, :, pl.ds(pl.multiple_of(me_t * kv_width, 128), kv_width)]
    hid_copies = [to_replica(hid_all.at[0], hid_all, 0, k) for k in range(1, replicas)]
    up_q_copies = [to_replica(up_q, up_q_all, 1, k) for k in range(1, replicas)]
    up_kv_copies = [to_replica(kv_mine, up_kv_all, 2, k) for k in range(1, replicas)]
    up_o_copies = [to_replica(up_o, up_o_all, 3, k) for k in range(1, replicas)]
    for copy in hid_copies + up_q_copies + up_kv_copies:
        copy.start()
    up_q_all[0] = up_q[...]
    up_kv_all[0] = kv_mine[...]
    up_o_all[0] = up_o[...]

    down_copy.wait()
    for copy in hid_copies:
        copy.wait_recv()
    hid_rows = hid_all[...].reshape(replicas * tokens, depth)
    partial = dot_nt(hid_rows, down[...].reshape(3 * rank_share, depth))
    blank = jnp.zeros((replicas * tokens, 128 - 3 * rank_share), jnp.float32)
    part[...] = jnp.concatenate([partial, blank], axis=1).reshape(replicas, tokens, 128)
    part_copies = []
    for k in range(replicas):
        for m in range(shards):
            if k or m:
                back = (replicas - k) % replicas
                part_copies.append(
                    pltpu.make_async_remote_copy(
                        src_ref=part.at[k],
                        dst_ref=part_all.at[back, m],
                        send_sem=part_send.at[back, m],
                        recv_sem=part_recv.at[back, m],
                        device_id={
                            "replica": lax.rem(me_r + back, replicas),
                            "tensor": lax.rem(me_t + m, shards),
                        },
                        device_id_type=MESH,
                    )
                )
                part_copies[-1].start()
    part_all[0, 0] = part[0]

    down_o_copy.wait()
    down_o_all[0] = down_o[...]
    down_o_copies = [to_replica(down_o, down_o_all, 4, k) for k in range(1, replicas)]
    for copy in down_o_copies + up_o_copies:
        copy.start()

    for copy in part_copies:
        copy.wait_recv()
    ranks = []
    for k in range(replicas):
        total = part_all[k, 0]
        for m in range(1, shards):
            total = total + part_all[k, m]
        ranks.append(total.astype(jnp.bfloat16))

    def rank_of(p):
        return jnp.concatenate(
            [r[:, p * rank_share : (p + 1) * rank_share] for r in ranks], axis=1
        )

    for copy in up_q_copies + up_kv_copies:
        copy.wait_recv()
    queries = frozen_q[...].astype(jnp.float32) + ADAPTER_SCALING * jnp.dot(
        rank_of(0),
        up_q_all[...].reshape(replicas * rank_share, up_q.shape[1]),
        preferred_element_type=jnp.float32,
    )
    queries = queries.astype(jnp.bfloat16).astype(jnp.float32)
    for h in range(heads):
        q_heads[h] = queries[:, h * HD : (h + 1) * HD]
    group = HEADS // KV
    kv_columns = pl.ds(pl.multiple_of(me_t * kv_width, 128), kv_width)
    for p, target in ((0, k_heads), (1, v_heads)):
        up = jnp.concatenate([up_kv_all[k, p] for k in range(replicas)], axis=0)
        fresh = frozen_kv[p, :, kv_columns].astype(jnp.float32) + ADAPTER_SCALING * jnp.dot(
            rank_of(1 + p), up, preferred_element_type=jnp.float32
        )
        fresh = fresh.astype(jnp.bfloat16).astype(jnp.float32)
        for h in range(heads):
            g = h // group
            target[h] = fresh[:, g * HD : (g + 1) * HD]

    lines = steps * heads
    line_head = lax.rem(lax.broadcasted_iota(jnp.int32, (lines, HD), 0), heads)
    line_step = lax.broadcasted_iota(jnp.int32, (lines, 1), 0) // heads
    place = lax.broadcasted_iota(jnp.int32, (lines, slots), 1)
    root = 1.0 / math.sqrt(HD)

    def line(source, s, b):
        return source[:, pl.ds(s * rows + b, 1), :].reshape(heads, HD)

    def score_row(b):
        query = jnp.concatenate([line(q_heads, s, b) for s in range(steps)], axis=0)
        scores = None
        for h in range(0, heads, 2):
            left = jnp.concatenate(
                [jnp.where(line_head == h + i, query, 0.0) for i in range(2)], axis=1
            ).astype(jnp.bfloat16)
            pair = jnp.concatenate([keys[b, h], keys[b, h + 1]], axis=1)
            product = dot_nt(left, pair)
            scores = product if scores is None else scores + product
        return query, scores

    def weigh_row(b, query, scores):
        scores = jnp.where(place < lens[b], scores * root, NEG_FILL)
        highest = jnp.max(scores, axis=-1, keepdims=True)
        fresh_scores = []
        for t in range(steps):
            new_key = jnp.concatenate([line(k_heads, t, b)] * steps, axis=0)
            score = jnp.sum(query * new_key, axis=-1, keepdims=True) * root
            score = jnp.where(line_step >= t, score, NEG_FILL)
            fresh_scores.append(score)
            highest = jnp.maximum(highest, score)
        weights = jnp.exp(scores - highest)
        total = jnp.sum(weights, axis=-1, keepdims=True)
        fresh_exp = [jnp.exp(score - highest) for score in fresh_scores]
        for value in fresh_exp:
            total = total + value
        inverse = 1.0 / total
        probs = (weights * inverse).astype(jnp.bfloat16)
        mixed = jnp.zeros((lines, HD), jnp.float32)
        for t in range(steps):
            new_value = jnp.concatenate([line(v_heads, t, b)] * steps, axis=0)
            prob = (fresh_exp[t] * inverse).astype(jnp.bfloat16).astype(jnp.float32)
            mixed = mixed + prob * new_value
        return probs, mixed

    def mix_row(b, probs, mixed):
        for h in range(0, heads, 2):
            pair = jnp.concatenate([values[b, h], values[b, h + 1]], axis=1)
            both = jnp.dot(probs, pair, preferred_element_type=jnp.float32)
            for i in range(2):
                mixed = mixed + jnp.where(
                    line_head == h + i, both[:, i * HD : (i + 1) * HD], 0.0
                )
        for s in range(steps):
            att_heads[:, pl.ds(s * rows + b, 1), :] = mixed[
                s * heads : (s + 1) * heads
            ].reshape(heads, 1, HD)

    together = math.gcd(rows, ROWS)

    @pl.loop(0, rows, step=together)
    def _(first):
        batch = [first + i for i in range(together)]
        for b in batch:
            key_copy(b).wait()
            value_copy(b).wait()
        scored = [score_row(b) for b in batch]
        weighed = [weigh_row(b, *of) for b, of in zip(batch, scored)]
        for b, of in zip(batch, weighed):
            mix_row(b, *of)

    attended = jnp.concatenate([att_heads[h] for h in range(heads)], axis=1).astype(jnp.bfloat16)

    for copy in down_o_copies:
        copy.wait_recv()
    low = dot_nt(attended, down_o_all[...].reshape(replicas * rank_share, depth))
    rank_total = replicas * rank_share
    rank_out[0] = jnp.concatenate(
        [low, jnp.zeros((tokens, 128 - rank_total), jnp.float32)], axis=1
    )
    rank_copies = [
        to_shard(rank_out.at[0], rank_out.at[m], rank_send.at[m], rank_recv.at[m], m)
        for m in range(1, shards)
    ]
    for copy in rank_copies:
        copy.start()

    def sum_copy(m, c):
        return to_shard(
            sums_out.at[m, c], sums_in.at[m, c], sum_send.at[m, c], sum_recv.at[m, c], m
        )

    for spot, m in enumerate(order):
        base = (spot % held) * chunks

        @pl.loop(0, chunks)
        def _(c, m=m, spot=spot, base=base):
            weight_copy(m, c, base + c).wait()
            product = jnp.dot(attended, wbuf[base + c], preferred_element_type=jnp.float32)
            if m:
                sums_out[m, c] = product.astype(jnp.bfloat16)
                sum_copy(m, c).start()
            else:
                own[c] = product
            if spot + held < shards:
                weight_copy(order[spot + held], c, base + c).start()

    for copy in rank_copies + up_o_copies:
        copy.wait_recv()
    rank_sum = rank_out[0]
    for m in range(1, shards):
        rank_sum = rank_sum + rank_out[m]
    rank_sum = rank_sum[:, :rank_total] * ADAPTER_SCALING
    rank_high = rank_sum.astype(jnp.bfloat16)
    rank_low = (rank_sum - rank_high.astype(jnp.float32)).astype(jnp.bfloat16)

    def full_copy(m, c):
        spot = me_t * chunks + c
        return to_shard(
            full.at[spot], full.at[spot], full_send.at[m, c], full_recv.at[m, c], m
        )

    for c in range(chunks):
        columns = slice(c * BLOCK, (c + 1) * BLOCK)
        up = jnp.concatenate([up_o_all[k, :, columns] for k in range(replicas)], axis=0)
        updated = jnp.dot(rank_high, up, preferred_element_type=jnp.float32) + jnp.dot(
            rank_low, up, preferred_element_type=jnp.float32
        )
        mine = pl.ds(pl.multiple_of(me_t * share + c * BLOCK, BLOCK), BLOCK)
        updated = updated + own[c] + hid[:, mine].astype(jnp.float32)
        for m in range(1, shards):
            sum_copy(m, c).wait_recv()
            updated = updated + sums_in[m, c].astype(jnp.float32)
        rounded = updated.astype(jnp.bfloat16)
        full[me_t * chunks + c] = rounded
        for m in range(1, shards):
            full_copy(m, c).start()

    def arrived(m, c):
        spot = lax.rem(me_t + shards - m, shards) * chunks + c
        return to_shard(
            full.at[spot], full.at[spot], full_send.at[m, c], full_recv.at[m, c], m
        )

    for c in range(chunks):
        for m in range(1, shards):
            arrived(m, c).wait_recv()

    for copy in (
        hid_copies + up_q_copies + up_kv_copies + up_o_copies + down_o_copies + part_copies
    ):
        copy.wait_send()
    for copy in rank_copies:
        copy.wait_send()
    for m in range(1, shards):
        for c in range(chunks):
            sum_copy(m, c).wait_send()
            full_copy(m, c).wait_send()


def norm_kernel(full, gain, res_out, norm_out):
    blocks, tokens, block_width = full.shape
    chunks = res_out.shape[1] // block_width
    first = lax.axis_index("tensor") * chunks
    for c in range(chunks):
        res_out[:, c * block_width : (c + 1) * block_width] = full[first + c]
    square = jnp.zeros((tokens, block_width), jnp.float32)
    for i in range(blocks):
        block = full[i].astype(jnp.float32)
        square = square + block * block
    mean = jnp.sum(square, axis=-1, keepdims=True) / (blocks * block_width)
    norm = lax.rsqrt(mean + EPSILON)
    gains = gain[...].astype(jnp.float32)
    for i in range(blocks):
        block = full[i].astype(jnp.float32) * norm
        for j in range(0, block_width, 128):
            line = (i * block_width + j) // 128
            norm_out[:, i * block_width + j : i * block_width + j + 128] = (
                block[:, j : j + 128] * gains[line : line + 1]
            ).astype(jnp.bfloat16)


def body_fused(
    hidden,
    frozen_query,
    frozen_key_value,
    cache_keys,
    cache_values,
    lengths,
    out_weight,
    down_qkv,
    query_up_factor,
    key_value_up_factor,
    output_down_factor,
    output_up_factor,
    norm_gain,
):
    replicas = lax.axis_size("replica")
    shards = lax.axis_size("tensor")
    steps, rows, width = hidden.shape
    tokens = steps * rows
    share = width // shards
    chunks = share // BLOCK
    head_count = cache_keys.shape[1]
    depth = out_weight.shape[0]
    rank_share = query_up_factor.shape[0]
    kv_width = key_value_up_factor.shape[2] // shards
    vmem = pl.BlockSpec(memory_space=pltpu.VMEM)
    smem = pl.BlockSpec(memory_space=pltpu.SMEM)
    hbm = pl.BlockSpec(memory_space=pl.ANY)
    bf16, f32 = jnp.bfloat16, jnp.float32
    dma = pltpu.SemaphoreType.DMA
    per_head = pltpu.VMEM((head_count, tokens, HD), f32)
    down_qkv = jnp.swapaxes(down_qkv, 1, 2)
    output_down_factor = output_down_factor.T
    full = pl.pallas_call(
        functools.partial(fused_kernel, steps, replicas, shards),
        out_shape=jax.ShapeDtypeStruct((shards * chunks, tokens, BLOCK), bf16),
        in_specs=[vmem] * 3 + [smem] + [vmem] * 3 + [hbm] * 5,
        out_specs=vmem,
        scratch_shapes=[
            pltpu.VMEM(cache_keys.shape, bf16),
            pltpu.VMEM(cache_values.shape, bf16),
            pltpu.VMEM((SLOTS, depth, BLOCK), bf16),
            pltpu.VMEM(down_qkv.shape, bf16),
            pltpu.VMEM(output_down_factor.shape, bf16),
            pltpu.VMEM((replicas, tokens, depth), bf16),
            pltpu.VMEM((replicas, rank_share, depth), bf16),
            pltpu.VMEM((replicas, 2, rank_share, kv_width), bf16),
            pltpu.VMEM((replicas, rank_share, share), bf16),
            pltpu.VMEM((replicas, rank_share, depth), bf16),
            pltpu.VMEM((replicas, tokens, 128), f32),
            pltpu.VMEM((replicas, shards, tokens, 128), f32),
            per_head,
            per_head,
            per_head,
            per_head,
            pltpu.VMEM((shards, chunks, tokens, BLOCK), bf16),
            pltpu.VMEM((shards, chunks, tokens, BLOCK), bf16),
            pltpu.VMEM((chunks, tokens, BLOCK), f32),
            pltpu.VMEM((shards, tokens, 128), f32),
            dma((2, rows)),
            dma((SLOTS,)),
            dma((2,)),
            dma((5, replicas)),
            dma((5, replicas)),
            dma((replicas, shards)),
            dma((replicas, shards)),
            dma((shards, chunks)),
            dma((shards, chunks)),
            dma((shards,)),
            dma((shards,)),
            dma((shards, chunks)),
            dma((shards, chunks)),
        ],
        compiler_params=pltpu.CompilerParams(
            collective_id=0, has_side_effects=True, vmem_limit_bytes=62 * 2**20
        ),
    )(
        hidden.reshape(tokens, width),
        frozen_query.reshape(tokens, frozen_query.shape[2]),
        frozen_key_value.reshape(2, tokens, frozen_key_value.shape[3]),
        lengths,
        query_up_factor,
        key_value_up_factor,
        output_up_factor,
        down_qkv,
        output_down_factor,
        cache_keys,
        cache_values,
        out_weight,
    )
    residual, normed = pl.pallas_call(
        norm_kernel,
        out_shape=(
            jax.ShapeDtypeStruct((tokens, share), bf16),
            jax.ShapeDtypeStruct((tokens, width), bf16),
        ),
        in_specs=[vmem, vmem],
        out_specs=(vmem, vmem),
    )(full, norm_gain.reshape(width // 128, 128))
    return residual.reshape(steps, rows, share), normed.reshape(steps, rows, width)


def solution(mesh):
    in_specs = (
        P(None, ("groups", "replica"), None),
        P(None, ("groups", "replica"), "tensor"),
        P(None, None, ("groups", "replica"), None),
        P(("groups", "replica"), "tensor", None, None),
        P(("groups", "replica"), "tensor", None, None),
        P(("groups", "replica")),
        P("tensor", None),
        P("groups", "tensor", "replica"),
        P(("groups", "replica"), "tensor"),
        P(None, ("groups", "replica"), None),
        P(("groups", "tensor"), "replica"),
        P(("groups", "replica"), "tensor"),
        P(),
    )
    out_specs = (P(None, ("groups", "replica"), "tensor"), P(None, ("groups", "replica"), None))
    chosen = body_fused if fits(mesh) else body
    return jax.shard_map(chosen, mesh=mesh, in_specs=in_specs, out_specs=out_specs, check_vma=False)
```
